32 devices in a mesh: groups: 2 (over y), samples: 8 (over z, x), features: 2 (over core).
Axes of the slice: x: 2, y: 2, z: 4, core: 2. Of those that a mesh axis runs over, the one named last changes fastest.
Arguments:
- blocks: bfloat16 [720, 8, 128, 128], P(('groups', 'samples'), 'features'), parts along dimension 0, may hold values from -0.15625 to 0.15625
- block_cols: int32 [720, 8], P(('groups', 'samples'), 'features'), parts along dimension 0, may hold values from 0 to 255, as said below
- right_side: float32 [65536, 128], P(('groups', 'samples', 'features')), parts along dimension 0, may hold values from -6 to 6
- lambdas: float32 [128], replicated, may hold values from 0.1 to 1.5
Outputs:
- solution: float32 [65536, 128], P(('groups', 'samples', 'features')), parts along dimension 0
- residual: float32 [65536, 128], P(('groups', 'samples', 'features')), parts along dimension 0
The draws below stay inside these ranges and needn't reach their ends.
There are 2 independent parts, one for each index of `groups`. The reference program is written for one: setup_inputs(seed, part) draws one part's arguments, and reference() takes and returns one part's arrays. A program takes and returns all parts, laid end to end along the dimension named above; an argument that names none is the same for every part. Nothing has to cross between parts.
Inputs may be any that keep to these rules, and one draw needn't show every extreme that they name: `block_cols`: each row block names 8 distinct feature blocks; entries e < 4 name blocks g with (g // 16) % 2 == 0, the other entries blocks with (g // 16) % 2 == 1.
All inputs are finite; a program needn't handle non-finite values.
Results may differ from the reference program's by a relative error of at most 0.0087.
Values may be sent and summed in bfloat16 or wider, within the bound.
A program may use at most 128 MiB of HBM per device.

```python
import math
import jax
import jax.numpy as jnp
from jax import lax

F = 32768
K = 128
BLK = 128
ITERS = 2
RB_DEV = 45
FB = 256
NNZ_OWN = 4
SB = 16
NRB = 360
ROWS = 46080
N_SAMPLES = 8


def draw_block_cols(key, part):
    key = jax.random.fold_in(key, 7)
    half_blocks = FB // 2
    scores = jax.random.randint(key, (NRB, 2, half_blocks), 0, 1 << 20) * half_blocks + jnp.arange(half_blocks, dtype=jnp.int32)[None, None, :]
    forced = jnp.zeros((NRB, 2, half_blocks), jnp.int32).at[0, 0, 0].set(1).at[0, 1, half_blocks - 1].set(1)
    scores = scores - forced * (1 << 30)
    chosen = jnp.argsort(scores, axis=-1)[:, :, :NNZ_OWN].astype(jnp.int32)
    owner_bits = jnp.arange(2, dtype=jnp.int32)[None, :, None]
    global_blocks = (chosen // SB * 2 + owner_bits) * SB + chosen % SB
    return global_blocks.reshape(NRB, 2 * NNZ_OWN).astype(jnp.int32)


def level_of(key, extent, pieces, low, high):
    level = 1.0
    for dim, shards_of in pieces:
        draws = jax.random.uniform(jax.random.fold_in(jax.random.fold_in(key, 6), dim), (shards_of,), jnp.float32, low / len(pieces), high / len(pieces))
        level = level * jnp.repeat(jnp.exp(draws), extent[dim] // shards_of).reshape((-1,) + (1,) * (len(extent) - 1 - dim))
    return level


def bell_draw(rng, dims, spread, limit, cuts=(), kind=jnp.bfloat16):
    gain = level_of(rng, dims, cuts, -0.22, 0.18) if cuts else 1.0
    result = jax.random.normal(rng, dims, jnp.float32) * spread * gain
    return jnp.minimum(jnp.maximum(result, -limit), limit).astype(kind)


def setup_inputs(seed: int = 0, part: int = 0) -> dict:
    key_list = jax.random.split(jax.random.key(seed), 5)
    own_keys = jax.random.split(jax.random.fold_in(key_list[4], part), 5)
    return {
        "blocks": bell_draw(own_keys[0], (NRB, 2 * NNZ_OWN, BLK, BLK), (ROWS // 32) ** -0.5, 0.15625, ((0, 8), (1, 2))),
        "block_cols": draw_block_cols(jax.random.fold_in(jax.random.fold_in(key_list[4], part), 71), part),
        "right_side": bell_draw(own_keys[2], (F, K), 1.0, 6.0, ((0, 16),), jnp.float32),
        "lambdas": jnp.clip(jnp.exp(jax.random.uniform(key_list[3], (K,), jnp.float32, math.log(0.1), math.log(1.5))), 0.1, 1.5),
    }


def apply_normal(direction, group_blocks, group_cols):
    direction_panel = direction.astype(jnp.bfloat16).reshape(FB, BLK, K)

    def sweep(running, group_item):
        these_blocks, these_cols = group_item
        wide_blocks = these_blocks.astype(jnp.float32)
        picked = direction_panel[these_cols].astype(jnp.float32)
        images = jnp.einsum('reij,rejk->rik', wide_blocks, picked)
        narrow = lax.optimization_barrier(images.astype(jnp.bfloat16)).astype(jnp.float32)
        back_terms = jnp.einsum('reij,rik->rejk', wide_blocks, narrow)
        running = running + jax.ops.segment_sum(back_terms.reshape(-1, BLK, K), these_cols.reshape(-1).astype(jnp.int32), num_segments=FB)
        return running, None

    running, _ = lax.scan(sweep, jnp.zeros((FB, BLK, K), jnp.float32), (group_blocks, group_cols))
    return running.reshape(F, K)


def reference(blocks, block_cols, right_side, lambdas):
    group_blocks = blocks.reshape(N_SAMPLES, RB_DEV, 2 * NNZ_OWN, BLK, BLK)
    group_cols = block_cols.reshape(N_SAMPLES, RB_DEV, 2 * NNZ_OWN)
    solution = jnp.zeros_like(right_side)
    residual = right_side
    direction = right_side
    norm_now = jnp.sum(residual * residual, axis=0)
    for iteration in range(ITERS):
        image = apply_normal(direction, group_blocks, group_cols) + lambdas[None, :] * direction
        step_size = norm_now / jnp.sum(direction * image, axis=0)
        solution = solution + step_size[None, :] * direction
        residual = residual - step_size[None, :] * image
        norm_next = jnp.sum(residual * residual, axis=0)
        direction = residual + (norm_next / norm_now)[None, :] * direction
        norm_now = norm_next
    return solution, residual
```

```python
import functools

import jax
import jax.numpy as jnp
from jax import lax
from jax.experimental import pallas as pl
from jax.experimental.pallas import tpu as pltpu
from jax.sharding import PartitionSpec as P

ITERS = 2
MESH = pl.DeviceIdType.MESH
F32 = jnp.float32
BF16 = jnp.bfloat16


def row_length(n):
    return 1 << ((n.bit_length() - 1) // 3)


def fold(a):
    return jnp.sum(a.reshape(-1, 8, a.shape[-1]), axis=0)


def kernel(
    n, X, SB,
    slots, prev, last, blocks_hbm, right, lam,
    sol, res,
    blocks, panel, img, imr, low, chain, acc, xs, xr, zs, zr, p, q,
    core_buf, all_buf,
    blk_sem, agz_s, agz_r, agx_s, agx_r, ft_s, ft_r, rsx_s, rsx_r, rsz_s, rsz_r,
    co_s, co_r, ar_s, ar_r,
):
    Z = n // X
    RB, E = blocks.shape[0], blocks.shape[1]
    CH = RB // img_chunks(RB)
    me = lax.axis_index("samples")
    core = lax.axis_index("features")
    z, x = me // X, me % X

    load = pltpu.make_async_copy(blocks_hbm, blocks, blk_sem)
    load.start()

    barrier = pltpu.get_barrier_semaphore()
    pl.semaphore_signal(barrier, inc=1, device_id={"features": 1 - core}, device_id_type=MESH)

    @pl.loop(1, n)
    def _(d):
        pl.semaphore_signal(
            barrier, inc=1, device_id={"samples": (me + d) % n}, device_id_type=MESH
        )

    def to(src, dst, ss, rs, **where):
        return pltpu.make_async_remote_copy(
            src_ref=src, dst_ref=dst, send_sem=ss, recv_sem=rs,
            device_id=where, device_id_type=MESH,
        )

    def shard(t, xx):
        return panel.at[pl.ds((t * X + xx) * SB, SB)]

    def gather(it):
        def zcopy(t, d):
            return to(shard(t, x), shard(t, x), agz_s.at[it, d, t], agz_r.at[it, t],
                      samples=me + (X if d == 0 else -X))

        def xcopy(t, dx, src_x):
            return to(shard(t, src_x), shard(t, src_x), agx_s.at[it, dx - 1, t],
                      agx_r.at[it, dx - 1, t], samples=z * X + (x + dx) % X)

        def send_x(t):
            for dx in range(1, X):
                xcopy(t, dx, x).start()

        for k in range(Z):
            for d in (0, 1):
                if k == 0 and d == 1:
                    continue
                t = z - k if d == 0 else z + k
                ok = (t >= 0) if d == 0 else (t < Z)

                def step(t=t, d=d):
                    if k:
                        zcopy(t, d).wait_recv()
                    for dd in ((0, 1) if k == 0 else (d,)):
                        pl.when((z + 1 < Z) if dd == 0 else (z > 0))(
                            lambda dd=dd: zcopy(t, dd).start())
                    send_x(t)

                if k:
                    pl.when(ok)(step)
                else:
                    step()
        for t in range(Z):
            for dx in range(1, X):
                xcopy(t, dx, (x - dx + X) % X).wait_recv()
        for t in range(Z):
            for dx in range(1, X):
                xcopy(t, dx, x).wait_send()
            pl.when((t <= z) & (z + 1 < Z))(lambda t=t: zcopy(t, 0).wait_send())
            pl.when((t >= z) & (z > 0))(lambda t=t: zcopy(t, 1).wait_send())

    def products(it):
        def part(c):
            rows = pl.ds(c * CH, CH)
            return to(img.at[rows], imr.at[rows], ft_s.at[it, c], ft_r.at[it, c],
                      features=1 - core)

        for c in range(RB // CH):
            @pl.loop(c * CH, (c + 1) * CH)
            def _(r):
                lhs = jnp.concatenate([blocks[r, e] for e in range(E)], axis=1)
                rhs = jnp.concatenate([panel[slots[r * E + e]] for e in range(E)], axis=0)
                img[r] = jnp.dot(lhs, rhs, preferred_element_type=F32)

            part(c).start()
        for c in range(RB // CH):
            part(c).wait_recv()

            @pl.loop(c * CH, (c + 1) * CH)
            def _(r):
                narrow = (img[r] + imr[r]).astype(BF16)
                for e in range(E):
                    term = lax.dot_general(
                        blocks[r, e], narrow, (((0,), (0,)), ((), ())),
                        preferred_element_type=F32)
                    i = r * E + e
                    chain[i + 1] = term + chain[prev[i]]

        for c in range(RB // CH):
            part(c).wait_send()

    def scatter(it):
        def xcopy(t, dx):
            return to(xs.at[dx - 1, t], xr.at[dx - 1, t], rsx_s.at[it, dx - 1, t],
                      rsx_r.at[it, dx - 1, t], samples=z * X + (x + dx) % X)

        def zcopy(t, d):
            return to(zs.at[t], zr.at[d, t], rsz_s.at[it, t], rsz_r.at[it, d, t],
                      samples=me + X - 2 * X * d)

        order = []
        a, b = z * 0, z * 0 + Z - 1
        for k in range(Z):
            low_end = (z - a > b - z).astype(jnp.int32)
            order.append(a * low_end + b * (1 - low_end))
            a = a + low_end
            b = b - (1 - low_end)

        for t in order:
            for dx in range(1, X):
                base = (t * X + (x + dx) % X) * SB

                @pl.loop(0, SB)
                def _(w):
                    xs[dx - 1, t, w] = chain[last[base + w]].astype(BF16)

                xcopy(t, dx).start()
        for t in order:
            base = (t * X + x) * SB

            @pl.loop(0, SB)
            def _(w):
                acc[t, w] = chain[last[base + w]]

        for k, t in enumerate(order):
            for dx in range(1, X):
                xcopy(t, dx).wait_recv()

            if k < Z - 1:
                d = (t < z).astype(jnp.int32)
                relay = ((t > z) & (z > 0)) | ((t < z) & (z + 1 < Z))
                pl.when(relay)(lambda: zcopy(t, d).wait_recv())
                more = relay.astype(jnp.int32)

                @pl.when(relay)
                def _():
                    @pl.loop(0, SB)
                    def _(w):
                        total = acc[t, w] + zr[d, t, w].astype(F32)
                        for dx in range(1, X):
                            total = total + xr[dx - 1, t, w].astype(F32)
                        zs[t, w] = total.astype(BF16)

                @pl.when(more == 0)
                def _():
                    @pl.loop(0, SB)
                    def _(w):
                        total = acc[t, w]
                        for dx in range(1, X):
                            total = total + xr[dx - 1, t, w].astype(F32)
                        zs[t, w] = total.astype(BF16)

                zcopy(t, d).start()
            else:
                @pl.loop(0, SB)
                def _(w):
                    total = acc[z, w]
                    for dx in range(1, X):
                        total = total + xr[dx - 1, z, w].astype(F32)
                    q[w] = total

        def arrive(d):
            zcopy(z, d).wait_recv()

            @pl.loop(0, SB)
            def _(w):
                q[w] = q[w] + zr[d, z, w].astype(F32)

        pl.when(z > 0)(lambda: arrive(0))
        pl.when(z + 1 < Z)(lambda: arrive(1))
        for t in range(Z):
            for dx in range(1, X):
                xcopy(t, dx).wait_send()
            pl.when(t != z)(lambda t=t: zcopy(t, 0).wait_send())

    def all_sum(a, j, values):
        m = len(values)
        rows = pl.ds(0, 8 * m)
        for i, v in enumerate(values):
            core_buf[j, 0, pl.ds(8 * i, 8)] = v
        cc = to(core_buf.at[j, 0, rows], core_buf.at[j, 1, rows], co_s.at[j], co_r.at[j],
                features=1 - core)
        cc.start()
        cc.wait()
        all_buf[j, me, rows] = core_buf[j, 0, rows] + core_buf[j, 1, rows]

        def copy(d):
            return to(all_buf.at[j, me, rows], all_buf.at[j, me, rows], ar_s.at[j, d],
                      ar_r.at[j, d], samples=(me + d) % n)

        def incoming(d):
            src = (me - d + n) % n
            return to(all_buf.at[j, src, rows], all_buf.at[j, src, rows], ar_s.at[j, d],
                      ar_r.at[j, d], samples=(me + d) % n)

        @pl.loop(1, n)
        def _(d):
            copy(d).start()

        @pl.loop(1, n)
        def _(d):
            incoming(d).wait_recv()

        @pl.loop(1, n)
        def _(d):
            copy(d).wait_send()

        total = all_buf[j, 0, rows]
        for s in range(1, n):
            total = total + all_buf[j, s, rows]
        return [jnp.sum(total[8 * i:8 * i + 8], axis=0, keepdims=True) for i in range(m)]

    zero = jnp.zeros((8, right.shape[-1]), F32)
    for w in range(SB):
        panel[me * SB + w] = right[w].astype(BF16)
    pl.semaphore_wait(barrier, n)
    gather(0)
    chain[0] = jnp.zeros(chain.shape[1:], F32)
    load.wait()
    norm = None
    for it in range(ITERS):
        final = it == ITERS - 1
        direction = right if it == 0 else p
        residual = right if it == 0 else res
        products(it)
        scatter(it)

        def curve(w, carry):
            dot, sq = carry
            v = direction[w]
            image = q[w] + lam[...] * v
            q[w] = image
            return dot + fold(v * image), sq + fold(v * v)

        dot, sq = lax.fori_loop(0, SB, curve, (zero, zero))
        if it == 0:
            norm, curvature = all_sum(None, 0, [sq, dot])
        else:
            (curvature,) = all_sum(None, 2 * it, [dot])
        step = norm / curvature

        def update(w, carry):
            v = direction[w]
            sol[w] = step * v if it == 0 else sol[w] + step * v
            new = residual[w] - step * q[w]
            res[w] = new
            return carry + fold(new * new)

        sq = lax.fori_loop(0, SB, update, zero)
        if not final:
            (norm_next,) = all_sum(None, 2 * it + 1, [sq])
            ratio = norm_next / norm
            norm = norm_next

            @pl.loop(0, SB)
            def _(w):
                v = res[w] + ratio * direction[w]
                p[w] = v
                panel[me * SB + w] = v.astype(BF16)

            gather(it + 1)


def img_chunks(rb):
    return max(d for d in range(1, 6) if rb % d == 0)


def per_device(n, blocks, block_cols, right_side, lambdas):
    RB, E, B, _ = blocks.shape
    K = right_side.shape[1]
    SB = right_side.shape[0] // B
    X = row_length(n)
    Z = n // X
    slots = (block_cols // (2 * SB) * SB + block_cols % SB).reshape(-1)
    entries = jnp.arange(RB * E, dtype=jnp.int32)
    same = (slots[:, None] == slots[None, :]) & (entries[None, :] < entries[:, None])
    prev = jnp.max(jnp.where(same, entries[None, :] + 1, 0), axis=1)
    hit = slots[None, :] == jnp.arange(n * SB, dtype=jnp.int32)[:, None]
    last = jnp.max(jnp.where(hit, entries[None, :] + 1, 0), axis=1)
    C = img_chunks(RB)
    dma = pltpu.SemaphoreType.DMA
    J = 2 * ITERS
    smem = pl.BlockSpec(memory_space=pltpu.SMEM)
    vmem = pl.BlockSpec(memory_space=pltpu.VMEM)
    sol, res = pl.pallas_call(
        functools.partial(kernel, n, X, SB),
        out_shape=[jax.ShapeDtypeStruct((SB, B, K), F32)] * 2,
        in_specs=[smem, smem, smem, pl.BlockSpec(memory_space=pl.ANY), vmem, vmem],
        out_specs=[vmem, vmem],
        scratch_shapes=[
            pltpu.VMEM((RB, E, B, B), BF16),
            pltpu.VMEM((n * SB, B, K), BF16),
            pltpu.VMEM((RB, B, K), F32),
            pltpu.VMEM((RB, B, K), F32),
            pltpu.VMEM((1, 16, K), BF16),
            pltpu.VMEM((RB * E + 1, B, K), F32),
            pltpu.VMEM((Z, SB, B, K), F32),
            pltpu.VMEM((X - 1, Z, SB, B, K), BF16),
            pltpu.VMEM((X - 1, Z, SB, B, K), BF16),
            pltpu.VMEM((Z, SB, B, K), BF16),
            pltpu.VMEM((2, Z, SB, B, K), BF16),
            pltpu.VMEM((SB, B, K), F32),
            pltpu.VMEM((SB, B, K), F32),
            pltpu.VMEM((J, 2, 16, K), F32),
            pltpu.VMEM((J, n, 16, K), F32),
            dma,
            dma((ITERS, 2, Z)), dma((ITERS, Z)),
            dma((ITERS, X - 1, Z)), dma((ITERS, X - 1, Z)),
            dma((ITERS, C)), dma((ITERS, C)),
            dma((ITERS, X - 1, Z)), dma((ITERS, X - 1, Z)),
            dma((ITERS, Z)), dma((ITERS, 2, Z)),
            dma((J,)), dma((J,)), dma((J, n)), dma((J, n)),
        ],
        compiler_params=pltpu.CompilerParams(
            collective_id=0, has_side_effects=True, vmem_limit_bytes=60 * 2**20),
    )(slots, prev, last, blocks, right_side.reshape(SB, B, K), lambdas.reshape(1, K))
    return sol.reshape(right_side.shape), res.reshape(right_side.shape)


def solution(mesh):
    in_specs = (
        P(("groups", "samples"), "features", None, None),
        P(("groups", "samples"), "features"),
        P(("groups", "samples", "features"), None),
        P(),
    )
    out_specs = (
        P(("groups", "samples", "features"), None),
        P(("groups", "samples", "features"), None),
    )
    return jax.shard_map(
        functools.partial(per_device, mesh.shape["samples"]),
        mesh=mesh, in_specs=in_specs, out_specs=out_specs, check_vma=False,
    )
```

```python
import functools

import jax
import jax.numpy as jnp
from jax import lax
from jax.experimental import pallas as pl
from jax.experimental.pallas import tpu as pltpu
from jax.sharding import PartitionSpec as P

ITERS = 2
MESH = pl.DeviceIdType.MESH
F32 = jnp.float32
BF16 = jnp.bfloat16


def row_length(n):
    return 1 << ((n.bit_length() - 1) // 3)


def fold(a):
    return jnp.sum(a.reshape(-1, 8, a.shape[-1]), axis=0)


def kernel(
    n, X, SB,
    slots, prev, last, blocks_hbm, right, lam,
    sol, res,
    blocks, panel, img, imr, chain, acc, xs, xr, zs, zr, es, er, p, q, all_buf,
    blk_sem, agz_s, agz_r, agx_s, agx_r, age_s, age_r, ft_s, ft_r,
    rsx_s, rsx_r, rsz_s, rsz_r, rse_s, rse_r, ar_s, ar_r,
):
    Z = n // X
    RB, E, B = blocks.shape[:3]
    CH = RB // img_chunks(RB)
    me = lax.axis_index("samples")
    core = lax.axis_index("features")
    z, x = me // X, me % X

    load = pltpu.make_async_copy(blocks_hbm, blocks, blk_sem)
    load.start()

    barrier = pltpu.get_barrier_semaphore()
    mine = me * 2 + core

    @pl.loop(1, 2 * n)
    def _(d):
        other = (mine + d) % (2 * n)
        pl.semaphore_signal(
            barrier, inc=1, device_id={"samples": other // 2, "features": other % 2},
            device_id_type=MESH)

    def to(src, dst, ss, rs, **where):
        return pltpu.make_async_remote_copy(
            src_ref=src, dst_ref=dst, send_sem=ss, recv_sem=rs,
            device_id=where, device_id_type=MESH,
        )

    HS = SB // 2
    zp = z + 1 - 2 * (z % 2)
    peer = me + X - 2 * X * (z % 2)

    def half(h):
        return pl.ds(h * HS, HS)

    def piece(t, xx, h):
        return panel.at[pl.ds((t * X + xx) * SB + h * HS, HS)]

    def gather(it):
        def zcopy(t, h, d):
            return to(piece(t, x, h), piece(t, x, h), agz_s.at[it, d, t, h],
                      agz_r.at[it, t, h], samples=me + (X if d == 0 else -X))

        def xcopy(t, h, dx, src_x):
            return to(piece(t, src_x, h), piece(t, src_x, h), agx_s.at[it, dx - 1, t, h],
                      agx_r.at[it, dx - 1, t, h], samples=z * X + (x + dx) % X)

        def ecopy(t, dx):
            ref = piece(t, (x - dx + X) % X, 1)
            return to(ref, ref, age_s.at[it, dx - 1], age_r.at[it, dx - 1], samples=peer)

        def send_x(t, h):
            for dx in range(1, X):
                xcopy(t, h, dx, x).start()

        for h in (0, 1):
            for d in (0, 1):
                pl.when((z + 1 < Z) if d == 0 else (z > 0))(
                    lambda h=h, d=d: zcopy(z, h, d).start())
            send_x(z, h)
        for k in range(1, Z):
            for h in (0, 1):
                for d in (0, 1):
                    t = z - k if d == 0 else z + k

                    @pl.when((t >= 0) if d == 0 else (t < Z))
                    def _(t=t, h=h, d=d, k=k):
                        zcopy(t, h, d).wait_recv()
                        pl.when((z + 1 < Z) if d == 0 else (z > 0))(
                            lambda: zcopy(t, h, d).start())
                        if k == 1 and h == 1:
                            pl.when(t != zp)(lambda: send_x(t, h))
                        else:
                            send_x(t, h)
            if k == 1:
                for dx in range(1, X):
                    xcopy(z, 1, dx, (x - dx + X) % X).wait_recv()
                    ecopy(z, dx).start()
        for t in range(Z):
            for dx in range(1, X):
                xcopy(t, 0, dx, (x - dx + X) % X).wait_recv()
                pl.when((t != zp) & (t != z))(
                    lambda t=t, dx=dx: xcopy(t, 1, dx, (x - dx + X) % X).wait_recv())
        for dx in range(1, X):
            ecopy(zp, dx).wait_recv()
        for t in range(Z):
            for dx in range(1, X):
                xcopy(t, 0, dx, x).wait_send()
                pl.when(t != zp)(lambda t=t, dx=dx: xcopy(t, 1, dx, x).wait_send())
            for h in (0, 1):
                pl.when((t <= z) & (z + 1 < Z))(lambda t=t, h=h: zcopy(t, h, 0).wait_send())
                pl.when((t >= z) & (z > 0))(lambda t=t, h=h: zcopy(t, h, 1).wait_send())
        for dx in range(1, X):
            ecopy(z, dx).wait_send()

    def products(it):
        def part(c):
            rows = pl.ds(c * CH, CH)
            return to(img.at[rows], imr.at[rows], ft_s.at[it, c], ft_r.at[it, c],
                      features=1 - core)

        U = 3 if CH % 3 == 0 else 1

        for c in range(RB // CH):
            @pl.loop(c * CH, (c + 1) * CH, step=U)
            def _(r0):
                for u in range(U):
                    r = r0 + u
                    lhs = jnp.concatenate([blocks[r, e] for e in range(E)], axis=1)
                    rhs = jnp.concatenate([panel[slots[r * E + e]] for e in range(E)], axis=0)
                    img[r] = jnp.dot(lhs, rhs, preferred_element_type=F32)

            part(c).start()
        for c in range(RB // CH):
            part(c).wait_recv()

            @pl.loop(c * CH, (c + 1) * CH, step=U)
            def _(r0):
                terms = []
                for u in range(U):
                    r = r0 + u
                    narrow = (img[r] + imr[r]).astype(BF16)
                    wide = jnp.concatenate([blocks[r, e] for e in range(E)], axis=1)
                    terms.append(lax.dot_general(
                        wide, narrow, (((0,), (0,)), ((), ())), preferred_element_type=F32))
                for u in range(U):
                    for e in range(E):
                        i = (r0 + u) * E + e
                        chain[i + 1] = terms[u][e * B:(e + 1) * B] + chain[prev[i]]

        for c in range(RB // CH):
            part(c).wait_send()

    def scatter(it):
        def xcopy(t, h, dx):
            return to(xs.at[dx - 1, t, half(h)], xr.at[dx - 1, t, half(h)],
                      rsx_s.at[it, dx - 1, t, h], rsx_r.at[it, dx - 1, t, h],
                      samples=z * X + (x + dx) % X)

        def zcopy(t, h, d):
            return to(zs.at[t, half(h)], zr.at[d, t, half(h)], rsz_s.at[it, t, h],
                      rsz_r.at[it, d, t, h], samples=me + X - 2 * X * d)

        def ecopy(dx):
            return to(es.at[dx - 1], er.at[dx - 1], rse_s.at[it, dx - 1],
                      rse_r.at[it, dx - 1], samples=peer)

        def term(t, xx, w):
            return chain[last[(t * X + xx) * SB + w]]

        order = []
        a, b = z * 0, z * 0 + Z - 1
        for k in range(Z):
            low_end = (z - a > b - z).astype(jnp.int32)
            order.append(a * low_end + b * (1 - low_end))
            a = a + low_end
            b = b - (1 - low_end)

        def send_x(t, h, dx, extra=False):
            xx = (x + dx) % X

            @pl.loop(0, HS)
            def _(v):
                w = v + h * HS
                total = term(t, xx, w)
                if extra:
                    total = total + er[dx - 1, v].astype(F32)
                xs[dx - 1, t, w] = total.astype(BF16)

            xcopy(t, h, dx).start()

        def send_extra():
            for dx in range(1, X):
                @pl.loop(0, HS)
                def _(v):
                    es[dx - 1, v] = term(zp, (x + dx) % X, v + HS).astype(BF16)

                ecopy(dx).start()

        for k, t in enumerate(order):
            for h in (0, 1):
                for dx in range(1, X):
                    if h == 0:
                        send_x(t, h, dx)
                    elif k < Z - 1:
                        pl.when(t != zp)(lambda t=t, dx=dx: send_x(t, 1, dx))
                    else:
                        ecopy(dx).wait_recv()
                        send_x(t, h, dx, True)
                if k == 0 and h == 0:
                    send_extra()
        for t in order:
            @pl.loop(0, SB)
            def _(w):
                acc[t, w] = term(t, x, w)

        def add_x(t, h):
            for dx in range(1, X):
                xcopy(t, h, dx).wait_recv()

            @pl.loop(h * HS, (h + 1) * HS)
            def _(w):
                total = acc[t, w]
                for dx in range(1, X):
                    total = total + xr[dx - 1, t, w].astype(F32)
                acc[t, w] = total

        def add_z(t, h, d):
            zcopy(t, h, d).wait_recv()

            @pl.loop(h * HS, (h + 1) * HS)
            def _(w):
                acc[t, w] = acc[t, w] + zr[d, t, w].astype(F32)

        for k, t in enumerate(order):
            for h in (0, 1):
                if h == 1 and k < Z - 1:
                    pl.when(t != zp)(lambda t=t: add_x(t, 1))
                else:
                    add_x(t, h)
                if k == Z - 1:
                    pl.when(z > 0)(lambda t=t, h=h: add_z(t, h, 0))
                    pl.when(z + 1 < Z)(lambda t=t, h=h: add_z(t, h, 1))
                    continue
                d = (t < z).astype(jnp.int32)
                relay = ((t > z) & (z > 0)) | ((t < z) & (z + 1 < Z))
                pl.when(relay)(lambda t=t, h=h, d=d: add_z(t, h, d))

                @pl.loop(h * HS, (h + 1) * HS)
                def _(w):
                    zs[t, w] = acc[t, w].astype(BF16)

                zcopy(t, h, d).start()
        for t in range(Z):
            for dx in range(1, X):
                xcopy(t, 0, dx).wait_send()
                pl.when(t != zp)(lambda t=t, dx=dx: xcopy(t, 1, dx).wait_send())
            for h in (0, 1):
                pl.when(t != z)(lambda t=t, h=h: zcopy(t, h, 0).wait_send())
        for dx in range(1, X):
            ecopy(dx).wait_send()

    def all_sum(j, values):
        m = len(values)
        rows = pl.ds(0, 8 * m)
        for i, v in enumerate(values):
            all_buf[j, mine, pl.ds(8 * i, 8)] = v

        def copy(d, src):
            other = (mine + d) % (2 * n)
            return to(all_buf.at[j, src, rows], all_buf.at[j, src, rows], ar_s.at[j, d],
                      ar_r.at[j, d], samples=other // 2, features=other % 2)

        @pl.loop(1, 2 * n)
        def _(d):
            copy(d, mine).start()

        @pl.loop(1, 2 * n)
        def _(d):
            copy(d, (mine - d + 2 * n) % (2 * n)).wait_recv()

        @pl.loop(1, 2 * n)
        def _(d):
            copy(d, mine).wait_send()

        total = all_buf[j, 0, rows]
        for s in range(1, 2 * n):
            total = total + all_buf[j, s, rows]
        return [jnp.sum(total[8 * i:8 * i + 8], axis=0, keepdims=True) for i in range(m)]

    zero = jnp.zeros((8, right.shape[-1]), F32)
    for w in range(SB):
        panel[me * SB + w] = right[w].astype(BF16)
    pl.semaphore_wait(barrier, 2 * n - 1)
    gather(0)
    chain[0] = jnp.zeros(chain.shape[1:], F32)
    load.wait()
    norm = None
    for it in range(ITERS):
        final = it == ITERS - 1
        direction = right if it == 0 else p
        residual = right if it == 0 else res
        products(it)
        scatter(it)

        def curve(w, carry):
            dot, sq = carry
            v = direction[w]
            image = acc[z, w] + lam[...] * v
            q[w] = image
            return dot + fold(v * image), sq + fold(v * v)

        dot, sq = lax.fori_loop(0, SB, curve, (zero, zero))
        if it == 0:
            norm, curvature = all_sum(0, [sq, dot])
        else:
            (curvature,) = all_sum(2 * it, [dot])
        step = norm / curvature

        def update(w, carry):
            v = direction[w]
            sol[w] = step * v if it == 0 else sol[w] + step * v
            new = residual[w] - step * q[w]
            res[w] = new
            return carry + fold(new * new)

        sq = lax.fori_loop(0, SB, update, zero)
        if not final:
            (norm_next,) = all_sum(2 * it + 1, [sq])
            ratio = norm_next / norm
            norm = norm_next

            @pl.loop(0, SB)
            def _(w):
                v = res[w] + ratio * direction[w]
                p[w] = v
                panel[me * SB + w] = v.astype(BF16)

            gather(it + 1)


def img_chunks(rb):
    return max(d for d in range(1, 6) if rb % d == 0)


def per_device(n, blocks, block_cols, right_side, lambdas):
    RB, E, B, _ = blocks.shape
    K = right_side.shape[1]
    SB = right_side.shape[0] // B
    X = row_length(n)
    Z = n // X
    slots = (block_cols // (2 * SB) * SB + block_cols % SB).reshape(-1)
    entries = jnp.arange(RB * E, dtype=jnp.int32)
    same = (slots[:, None] == slots[None, :]) & (entries[None, :] < entries[:, None])
    prev = jnp.max(jnp.where(same, entries[None, :] + 1, 0), axis=1)
    hit = slots[None, :] == jnp.arange(n * SB, dtype=jnp.int32)[:, None]
    last = jnp.max(jnp.where(hit, entries[None, :] + 1, 0), axis=1)
    C = img_chunks(RB)
    dma = pltpu.SemaphoreType.DMA
    J = 2 * ITERS
    smem = pl.BlockSpec(memory_space=pltpu.SMEM)
    vmem = pl.BlockSpec(memory_space=pltpu.VMEM)
    sol, res = pl.pallas_call(
        functools.partial(kernel, n, X, SB),
        out_shape=[jax.ShapeDtypeStruct((SB, B, K), F32)] * 2,
        in_specs=[smem, smem, smem, pl.BlockSpec(memory_space=pl.ANY), vmem, vmem],
        out_specs=[vmem, vmem],
        scratch_shapes=[
            pltpu.VMEM((RB, E, B, B), BF16),
            pltpu.VMEM((n * SB, B, K), BF16),
            pltpu.VMEM((RB, B, K), F32),
            pltpu.VMEM((RB, B, K), F32),
            pltpu.VMEM((RB * E + 1, B, K), F32),
            pltpu.VMEM((Z, SB, B, K), F32),
            pltpu.VMEM((X - 1, Z, SB, B, K), BF16),
            pltpu.VMEM((X - 1, Z, SB, B, K), BF16),
            pltpu.VMEM((Z, SB, B, K), BF16),
            pltpu.VMEM((2, Z, SB, B, K), BF16),
            pltpu.VMEM((X - 1, SB // 2, B, K), BF16),
            pltpu.VMEM((X - 1, SB // 2, B, K), BF16),
            pltpu.VMEM((SB, B, K), F32),
            pltpu.VMEM((SB, B, K), F32),
            pltpu.VMEM((J, 2 * n, 16, K), F32),
            dma,
            dma((ITERS, 2, Z, 2)), dma((ITERS, Z, 2)),
            dma((ITERS, X - 1, Z, 2)), dma((ITERS, X - 1, Z, 2)),
            dma((ITERS, X - 1)), dma((ITERS, X - 1)),
            dma((ITERS, C)), dma((ITERS, C)),
            dma((ITERS, X - 1, Z, 2)), dma((ITERS, X - 1, Z, 2)),
            dma((ITERS, Z, 2)), dma((ITERS, 2, Z, 2)),
            dma((ITERS, X - 1)), dma((ITERS, X - 1)),
            dma((J, 2 * n)), dma((J, 2 * n)),
        ],
        compiler_params=pltpu.CompilerParams(
            collective_id=0, has_side_effects=True, vmem_limit_bytes=60 * 2**20),
    )(slots, prev, last, blocks, right_side.reshape(SB, B, K), lambdas.reshape(1, K))
    return sol.reshape(right_side.shape), res.reshape(right_side.shape)


def solution(mesh):
    in_specs = (
        P(("groups", "samples"), "features", None, None),
        P(("groups", "samples"), "features"),
        P(("groups", "samples", "features"), None),
        P(),
    )
    out_specs = (
        P(("groups", "samples", "features"), None),
        P(("groups", "samples", "features"), None),
    )
    return jax.shard_map(
        functools.partial(per_device, mesh.shape["samples"]),
        mesh=mesh, in_specs=in_specs, out_specs=out_specs, check_vma=False,
    )
```

```python
import functools

import jax
import jax.numpy as jnp
from jax import lax
from jax.experimental import pallas as pl
from jax.experimental.pallas import tpu as pltpu
from jax.sharding import PartitionSpec as P

ITERS = 2
MESH = pl.DeviceIdType.MESH
F32 = jnp.float32
BF16 = jnp.bfloat16


def row_length(n):
    return 1 << ((n.bit_length() - 1) // 3)


def fold(a):
    return jnp.sum(a.reshape(-1, 8, a.shape[-1]), axis=0)


def kernel(
    n, X, SB,
    slots, prev, last, blocks_hbm, right, lam,
    sol, res,
    blocks, panel, img, imr, chain, acc, xs, xr, zs, zr, es, er, p, images, all_buf,
    blk_sem, agz_s, agz_r, agx_s, agx_r, age_s, age_r, ft_s, ft_r,
    rsx_s, rsx_r, rsz_s, rsz_r, rse_s, rse_r, ar_s, ar_r,
):
    Z = n // X
    RB, E, B = blocks.shape[:3]
    CH = RB // img_chunks(RB)
    me = lax.axis_index("samples")
    core = lax.axis_index("features")
    z, x = me // X, me % X

    load = pltpu.make_async_copy(blocks_hbm, blocks, blk_sem)
    load.start()

    barrier = pltpu.get_barrier_semaphore()
    mine = me * 2 + core

    @pl.loop(1, 2 * n)
    def _(d):
        other = (mine + d) % (2 * n)
        pl.semaphore_signal(
            barrier, inc=1, device_id={"samples": other // 2, "features": other % 2},
            device_id_type=MESH)

    def to(src, dst, ss, rs, **where):
        return pltpu.make_async_remote_copy(
            src_ref=src, dst_ref=dst, send_sem=ss, recv_sem=rs,
            device_id=where, device_id_type=MESH,
        )

    HS = SB // 2
    zero = jnp.zeros((8, right.shape[-1]), F32)
    zp = z + 1 - 2 * (z % 2)
    peer = me + X - 2 * X * (z % 2)

    def half(h):
        return pl.ds(h * HS, HS)

    def piece(t, xx, h):
        return panel.at[pl.ds((t * X + xx) * SB + h * HS, HS)]

    def gather(it, beside=None):
        def zcopy(t, h, d):
            return to(piece(t, x, h), piece(t, x, h), agz_s.at[it, d, t, h],
                      agz_r.at[it, t, h], samples=me + (X if d == 0 else -X))

        def xcopy(t, h, dx, src_x):
            return to(piece(t, src_x, h), piece(t, src_x, h), agx_s.at[it, dx - 1, t, h],
                      agx_r.at[it, dx - 1, t, h], samples=z * X + (x + dx) % X)

        def ecopy(t, dx):
            ref = piece(t, (x - dx + X) % X, 1)
            return to(ref, ref, age_s.at[it, dx - 1], age_r.at[it, dx - 1], samples=peer)

        def send_x(t, h):
            for dx in range(1, X):
                xcopy(t, h, dx, x).start()

        for h in (0, 1):
            for d in (0, 1):
                pl.when((z + 1 < Z) if d == 0 else (z > 0))(
                    lambda h=h, d=d: zcopy(z, h, d).start())
            send_x(z, h)
        if beside is not None:
            beside()
        for k in range(1, Z):
            for h in (0, 1):
                for d in (0, 1):
                    t = z - k if d == 0 else z + k

                    @pl.when((t >= 0) if d == 0 else (t < Z))
                    def _(t=t, h=h, d=d, k=k):
                        zcopy(t, h, d).wait_recv()
                        pl.when((z + 1 < Z) if d == 0 else (z > 0))(
                            lambda: zcopy(t, h, d).start())
                        if k == 1 and h == 1:
                            pl.when(t != zp)(lambda: send_x(t, h))
                        else:
                            send_x(t, h)
            if k == max(Z - 2, 1):
                for dx in range(1, X):
                    xcopy(z, 1, dx, (x - dx + X) % X).wait_recv()
                    ecopy(z, dx).start()
        for t in range(Z):
            for dx in range(1, X):
                xcopy(t, 0, dx, (x - dx + X) % X).wait_recv()
                pl.when((t != zp) & (t != z))(
                    lambda t=t, dx=dx: xcopy(t, 1, dx, (x - dx + X) % X).wait_recv())
        for dx in range(1, X):
            ecopy(zp, dx).wait_recv()
        for t in range(Z):
            for dx in range(1, X):
                xcopy(t, 0, dx, x).wait_send()
                pl.when(t != zp)(lambda t=t, dx=dx: xcopy(t, 1, dx, x).wait_send())
            for h in (0, 1):
                pl.when((t <= z) & (z + 1 < Z))(lambda t=t, h=h: zcopy(t, h, 0).wait_send())
                pl.when((t >= z) & (z > 0))(lambda t=t, h=h: zcopy(t, h, 1).wait_send())
        for dx in range(1, X):
            ecopy(z, dx).wait_send()

    def products(it, ratio_of=None):
        def part(c):
            rows = pl.ds(c * CH, CH)
            return to(img.at[rows], imr.at[rows], ft_s.at[it, c], ft_r.at[it, c],
                      features=1 - core)

        U = 3 if CH % 3 == 0 else 1

        for c in range(RB // CH):
            @pl.loop(c * CH, (c + 1) * CH, step=U)
            def _(r0):
                for u in range(U):
                    r = r0 + u
                    lhs = jnp.concatenate([blocks[r, e] for e in range(E)], axis=1)
                    rhs = jnp.concatenate([panel[slots[r * E + e]] for e in range(E)], axis=0)
                    img[r] = jnp.dot(lhs, rhs, preferred_element_type=F32)

            part(c).start()
        ratio = None if ratio_of is None else ratio_of()
        squares = zero
        for c in range(RB // CH):
            part(c).wait_recv()

            def back(g, squares):
                r0 = c * CH + g * U
                terms = []
                for u in range(U):
                    r = r0 + u
                    image = img[r] + imr[r]
                    if ratio is not None:
                        image = image + ratio * images[r]
                    if it < ITERS - 1:
                        images[r] = image
                    squares = squares + fold(image * image)
                    narrow = image.astype(BF16)
                    wide = jnp.concatenate([blocks[r, e] for e in range(E)], axis=1)
                    terms.append(lax.dot_general(
                        wide, narrow, (((0,), (0,)), ((), ())), preferred_element_type=F32))
                for u in range(U):
                    for e in range(E):
                        i = (r0 + u) * E + e
                        chain[i + 1] = terms[u][e * B:(e + 1) * B] + chain[prev[i]]
                return squares

            squares = lax.fori_loop(0, CH // U, back, squares)

        for c in range(RB // CH):
            part(c).wait_send()
        return jnp.where(core == 0, squares, zero), ratio

    def scatter(it):
        def xcopy(t, h, dx):
            return to(xs.at[dx - 1, t, half(h)], xr.at[dx - 1, t, half(h)],
                      rsx_s.at[it, dx - 1, t, h], rsx_r.at[it, dx - 1, t, h],
                      samples=z * X + (x + dx) % X)

        def zcopy(t, h, d):
            return to(zs.at[t, half(h)], zr.at[d, t, half(h)], rsz_s.at[it, t, h],
                      rsz_r.at[it, d, t, h], samples=me + X - 2 * X * d)

        def ecopy(dx):
            return to(es.at[dx - 1], er.at[dx - 1], rse_s.at[it, dx - 1],
                      rse_r.at[it, dx - 1], samples=peer)

        def term(t, xx, w):
            return chain[last[(t * X + xx) * SB + w]]

        order = []
        a, b = z * 0, z * 0 + Z - 1
        for k in range(Z):
            low_end = (z - a > b - z).astype(jnp.int32)
            order.append(a * low_end + b * (1 - low_end))
            a = a + low_end
            b = b - (1 - low_end)

        def send_x(t, h, dx, extra=False):
            xx = (x + dx) % X

            @pl.loop(0, HS)
            def _(v):
                w = v + h * HS
                total = term(t, xx, w)
                if extra:
                    total = total + er[dx - 1, v].astype(F32)
                xs[dx - 1, t, w] = total.astype(BF16)

            xcopy(t, h, dx).start()

        def send_extra():
            for dx in range(1, X):
                @pl.loop(0, HS)
                def _(v):
                    es[dx - 1, v] = term(zp, (x + dx) % X, v + HS).astype(BF16)

                ecopy(dx).start()

        for k, t in enumerate(order):
            for h in (0, 1):
                for dx in range(1, X):
                    if h == 0:
                        send_x(t, h, dx)
                    elif k < Z - 1:
                        pl.when(t != zp)(lambda t=t, dx=dx: send_x(t, 1, dx))
                    else:
                        ecopy(dx).wait_recv()
                        send_x(t, h, dx, True)
                if k == 0 and h == 0:
                    send_extra()
        for t in order:
            @pl.loop(0, SB)
            def _(w):
                acc[t, w] = term(t, x, w)

        def add_x(t, h):
            for dx in range(1, X):
                xcopy(t, h, dx).wait_recv()

            @pl.loop(h * HS, (h + 1) * HS)
            def _(w):
                total = acc[t, w]
                for dx in range(1, X):
                    total = total + xr[dx - 1, t, w].astype(F32)
                acc[t, w] = total

        def add_z(t, h, d):
            zcopy(t, h, d).wait_recv()

            @pl.loop(h * HS, (h + 1) * HS)
            def _(w):
                acc[t, w] = acc[t, w] + zr[d, t, w].astype(F32)

        for k, t in enumerate(order):
            for h in (0, 1):
                if h == 1 and k < Z - 1:
                    pl.when(t != zp)(lambda t=t: add_x(t, 1))
                else:
                    add_x(t, h)
                if k == Z - 1:
                    pl.when(z > 0)(lambda t=t, h=h: add_z(t, h, 0))
                    pl.when(z + 1 < Z)(lambda t=t, h=h: add_z(t, h, 1))
                    continue
                d = (t < z).astype(jnp.int32)
                relay = ((t > z) & (z > 0)) | ((t < z) & (z + 1 < Z))
                pl.when(relay)(lambda t=t, h=h, d=d: add_z(t, h, d))

                @pl.loop(h * HS, (h + 1) * HS)
                def _(w):
                    zs[t, w] = acc[t, w].astype(BF16)

                zcopy(t, h, d).start()
        for t in range(Z):
            for dx in range(1, X):
                xcopy(t, 0, dx).wait_send()
                pl.when(t != zp)(lambda t=t, dx=dx: xcopy(t, 1, dx).wait_send())
            for h in (0, 1):
                pl.when(t != z)(lambda t=t, h=h: zcopy(t, h, 0).wait_send())
        for dx in range(1, X):
            ecopy(dx).wait_send()

    def tile_copy(j, m, d, src):
        other = (mine + d) % (2 * n)
        rows = pl.ds(0, 8 * m)
        return to(all_buf.at[j, src, rows], all_buf.at[j, src, rows], ar_s.at[j, d],
                  ar_r.at[j, d], samples=other // 2, features=other % 2)

    def sum_start(j, values):
        for i, v in enumerate(values):
            all_buf[j, mine, pl.ds(8 * i, 8)] = v

        @pl.loop(1, 2 * n)
        def _(d):
            tile_copy(j, len(values), d, mine).start()

    def sum_finish(j, m):
        @pl.loop(1, 2 * n)
        def _(d):
            tile_copy(j, m, d, (mine - d + 2 * n) % (2 * n)).wait_recv()

        @pl.loop(1, 2 * n)
        def _(d):
            tile_copy(j, m, d, mine).wait_send()

        rows = pl.ds(0, 8 * m)
        total = all_buf[j, 0, rows]
        for s in range(1, 2 * n):
            total = total + all_buf[j, s, rows]
        return [jnp.sum(total[8 * i:8 * i + 8], axis=0, keepdims=True) for i in range(m)]

    for w in range(SB):
        panel[me * SB + w] = right[w].astype(BF16)
    pl.semaphore_wait(barrier, 2 * n - 1)
    gather(0)
    chain[0] = jnp.zeros(chain.shape[1:], F32)
    load.wait()
    norm = norm_next = None
    for it in range(ITERS):
        first, final = it == 0, it == ITERS - 1
        direction = right if first else p
        residual = right if first else res

        if first:
            squares, _ = products(it)
            own = lax.fori_loop(0, SB, lambda w, c: c + fold(right[w] * right[w]), zero)
            sum_start(0, [own, squares + lam[...] * own])
            scatter(it)
            norm, curvature = sum_finish(0, 2)
        else:
            def ratio_of():
                nonlocal norm, norm_next
                (norm_next,) = sum_finish(2 * it - 1, 1)
                return norm_next / norm

            squares, ratio = products(it, ratio_of)
            norm = norm_next
            before = right if it == 1 else p

            def turn(w, carry):
                v = res[w] + ratio * before[w]
                p[w] = v
                return carry + fold(v * v)

            own = lax.fori_loop(0, SB, turn, zero)
            sum_start(2 * it, [squares + lam[...] * own])
            scatter(it)
            (curvature,) = sum_finish(2 * it, 1)
        step = norm / curvature

        def update(w, carry):
            v = direction[w]
            sol[w] = step * v if first else sol[w] + step * v
            new = residual[w] - step * (acc[z, w] + lam[...] * v)
            res[w] = new
            if not final:
                panel[me * SB + w] = new.astype(BF16)
            return carry + fold(new * new)

        sq = lax.fori_loop(0, SB, update, zero)
        if not final:
            gather(it + 1, lambda: sum_start(2 * it + 1, [sq]))


def img_chunks(rb):
    return max(d for d in range(1, 6) if rb % d == 0)


def per_device(n, blocks, block_cols, right_side, lambdas):
    RB, E, B, _ = blocks.shape
    K = right_side.shape[1]
    SB = right_side.shape[0] // B
    X = row_length(n)
    Z = n // X
    slots = (block_cols // (2 * SB) * SB + block_cols % SB).reshape(-1)
    entries = jnp.arange(RB * E, dtype=jnp.int32)
    same = (slots[:, None] == slots[None, :]) & (entries[None, :] < entries[:, None])
    prev = jnp.max(jnp.where(same, entries[None, :] + 1, 0), axis=1)
    hit = slots[None, :] == jnp.arange(n * SB, dtype=jnp.int32)[:, None]
    last = jnp.max(jnp.where(hit, entries[None, :] + 1, 0), axis=1)
    C = img_chunks(RB)
    dma = pltpu.SemaphoreType.DMA
    J = 2 * ITERS
    smem = pl.BlockSpec(memory_space=pltpu.SMEM)
    vmem = pl.BlockSpec(memory_space=pltpu.VMEM)
    sol, res = pl.pallas_call(
        functools.partial(kernel, n, X, SB),
        out_shape=[jax.ShapeDtypeStruct((SB, B, K), F32)] * 2,
        in_specs=[smem, smem, smem, pl.BlockSpec(memory_space=pl.ANY), vmem, vmem],
        out_specs=[vmem, vmem],
        scratch_shapes=[
            pltpu.VMEM((RB, E, B, B), BF16),
            pltpu.VMEM((n * SB, B, K), BF16),
            pltpu.VMEM((RB, B, K), F32),
            pltpu.VMEM((RB, B, K), F32),
            pltpu.VMEM((RB * E + 1, B, K), F32),
            pltpu.VMEM((Z, SB, B, K), F32),
            pltpu.VMEM((X - 1, Z, SB, B, K), BF16),
            pltpu.VMEM((X - 1, Z, SB, B, K), BF16),
            pltpu.VMEM((Z, SB, B, K), BF16),
            pltpu.VMEM((2, Z, SB, B, K), BF16),
            pltpu.VMEM((X - 1, SB // 2, B, K), BF16),
            pltpu.VMEM((X - 1, SB // 2, B, K), BF16),
            pltpu.VMEM((SB, B, K), F32),
            pltpu.VMEM((RB, B, K), F32),
            pltpu.VMEM((J, 2 * n, 16, K), F32),
            dma,
            dma((ITERS, 2, Z, 2)), dma((ITERS, Z, 2)),
            dma((ITERS, X - 1, Z, 2)), dma((ITERS, X - 1, Z, 2)),
            dma((ITERS, X - 1)), dma((ITERS, X - 1)),
            dma((ITERS, C)), dma((ITERS, C)),
            dma((ITERS, X - 1, Z, 2)), dma((ITERS, X - 1, Z, 2)),
            dma((ITERS, Z, 2)), dma((ITERS, 2, Z, 2)),
            dma((ITERS, X - 1)), dma((ITERS, X - 1)),
            dma((J, 2 * n)), dma((J, 2 * n)),
        ],
        compiler_params=pltpu.CompilerParams(
            collective_id=0, has_side_effects=True, vmem_limit_bytes=60 * 2**20),
    )(slots, prev, last, blocks, right_side.reshape(SB, B, K), lambdas.reshape(1, K))
    return sol.reshape(right_side.shape), res.reshape(right_side.shape)


def solution(mesh):
    in_specs = (
        P(("groups", "samples"), "features", None, None),
        P(("groups", "samples"), "features"),
        P(("groups", "samples", "features"), None),
        P(),
    )
    out_specs = (
        P(("groups", "samples", "features"), None),
        P(("groups", "samples", "features"), None),
    )
    return jax.shard_map(
        functools.partial(per_device, mesh.shape["samples"]),
        mesh=mesh, in_specs=in_specs, out_specs=out_specs, check_vma=False,
    )
```

```python
import functools

import jax
import jax.numpy as jnp
from jax import lax
from jax.experimental import pallas as pl
from jax.experimental.pallas import tpu as pltpu
from jax.sharding import PartitionSpec as P

ITERS = 2
MESH = pl.DeviceIdType.MESH
F32 = jnp.float32
BF16 = jnp.bfloat16


def row_length(n):
    return 1 << ((n.bit_length() - 1) // 3)


def fold(a):
    return jnp.sum(a.reshape(-1, 8, a.shape[-1]), axis=0)


def kernel(
    n, X, SB,
    slots, prev, last, blocks_hbm, right, lam,
    sol, res,
    blocks, panel, img, imr, chain, acc, xs, xr, zs, zr, es, er, p, images, all_buf,
    blk_sem, agz_s, agz_r, agx_s, agx_r, age_s, age_r, ft_s, ft_r,
    rsx_s, rsx_r, rsz_s, rsz_r, rse_s, rse_r, ar_s, ar_r,
):
    Z = n // X
    RB, E, B = blocks.shape[:3]
    CH = img_rows(RB)
    me = lax.axis_index("samples")
    core = lax.axis_index("features")
    z, x = me // X, me % X

    load = pltpu.make_async_copy(blocks_hbm, blocks, blk_sem)
    load.start()

    barrier = pltpu.get_barrier_semaphore()
    mine = me * 2 + core

    @pl.loop(1, 2 * n)
    def _(d):
        other = (mine + d) % (2 * n)
        pl.semaphore_signal(
            barrier, inc=1, device_id={"samples": other // 2, "features": other % 2},
            device_id_type=MESH)

    def to(src, dst, ss, rs, **where):
        return pltpu.make_async_remote_copy(
            src_ref=src, dst_ref=dst, send_sem=ss, recv_sem=rs,
            device_id=where, device_id_type=MESH,
        )

    HS = SB // 2
    zero = jnp.zeros((8, right.shape[-1]), F32)
    zp = z + 1 - 2 * (z % 2)
    peer = me + X - 2 * X * (z % 2)

    def half(h):
        return pl.ds(h * HS, HS)

    def piece(t, xx, h):
        return panel.at[pl.ds((t * X + xx) * SB + h * HS, HS)]

    def gather(it, beside, late):
        def zcopy(t, h, d):
            return to(piece(t, x, h), piece(t, x, h), agz_s.at[it, d, t, h],
                      agz_r.at[it, t, h], samples=me + (X if d == 0 else -X))

        def xcopy(t, h, dx, src_x):
            return to(piece(t, src_x, h), piece(t, src_x, h), agx_s.at[it, dx - 1, t, h],
                      agx_r.at[it, dx - 1, t, h], samples=z * X + (x + dx) % X)

        def ecopy(t, dx):
            ref = piece(t, (x - dx + X) % X, 1)
            return to(ref, ref, age_s.at[it, dx - 1], age_r.at[it, dx - 1], samples=peer)

        def send_x(t, h):
            for dx in range(1, X):
                xcopy(t, h, dx, x).start()

        for h in (0, 1):
            for d in (0, 1):
                pl.when((z + 1 < Z) if d == 0 else (z > 0))(
                    lambda h=h, d=d: zcopy(z, h, d).start())
            send_x(z, h)
        beside()
        for k in range(1, Z):
            for h in (0, 1):
                for d in (0, 1):
                    t = z - k if d == 0 else z + k

                    @pl.when((t >= 0) if d == 0 else (t < Z))
                    def _(t=t, h=h, d=d, k=k):
                        zcopy(t, h, d).wait_recv()
                        pl.when((z + 1 < Z) if d == 0 else (z > 0))(
                            lambda: zcopy(t, h, d).start())
                        if k == 1 and h == 1:
                            pl.when(t != zp)(lambda: send_x(t, h))
                        else:
                            send_x(t, h)
            if k == max(Z - 2, 1):
                for dx in range(1, X):
                    xcopy(z, 1, dx, (x - dx + X) % X).wait_recv()
                    ecopy(z, dx).start()
        late()
        for t in range(Z):
            for dx in range(1, X):
                xcopy(t, 0, dx, (x - dx + X) % X).wait_recv()
                pl.when((t != zp) & (t != z))(
                    lambda t=t, dx=dx: xcopy(t, 1, dx, (x - dx + X) % X).wait_recv())
        for dx in range(1, X):
            ecopy(zp, dx).wait_recv()

        def drain():
            for t in range(Z):
                for dx in range(1, X):
                    xcopy(t, 0, dx, x).wait_send()
                    pl.when(t != zp)(lambda t=t, dx=dx: xcopy(t, 1, dx, x).wait_send())
                for h in (0, 1):
                    pl.when((t <= z) & (z + 1 < Z))(
                        lambda t=t, h=h: zcopy(t, h, 0).wait_send())
                    pl.when((t >= z) & (z > 0))(
                        lambda t=t, h=h: zcopy(t, h, 1).wait_send())
            for dx in range(1, X):
                ecopy(z, dx).wait_send()

        return drain

    def products(it, ratio, drain):
        def part(c):
            rows = pl.ds(c * CH, CH)
            return to(img.at[rows], imr.at[rows], ft_s.at[it, c], ft_r.at[it, c],
                      features=1 - core)

        @pl.loop(0, RB // CH)
        def _(c):
            for u in range(CH):
                r = c * CH + u
                lhs = jnp.concatenate([blocks[r, e] for e in range(E)], axis=1)
                rhs = jnp.concatenate([panel[slots[r * E + e]] for e in range(E)], axis=0)
                img[r] = jnp.dot(lhs, rhs, preferred_element_type=F32)
            part(c).start()

        drain()

        def back(c, squares):
            part(c).wait_recv()
            terms = []
            for u in range(CH):
                r = c * CH + u
                image = img[r] + imr[r]
                if ratio is not None:
                    image = image + ratio * images[r]
                if it < ITERS - 1:
                    images[r] = image
                squares = squares + fold(image * image)
                narrow = image.astype(BF16)
                wide = jnp.concatenate([blocks[r, e] for e in range(E)], axis=1)
                terms.append(lax.dot_general(
                    wide, narrow, (((0,), (0,)), ((), ())), preferred_element_type=F32))
            for u in range(CH):
                for e in range(E):
                    i = (c * CH + u) * E + e
                    chain[i + 1] = terms[u][e * B:(e + 1) * B] + chain[prev[i]]
            return squares

        squares = lax.fori_loop(0, RB // CH, back, zero)

        def sent():
            @pl.loop(0, RB // CH)
            def _(c):
                part(c).wait_send()

        return jnp.where(core == 0, squares, zero), sent

    def scatter(it, beside, late):
        def xcopy(t, h, dx):
            return to(xs.at[dx - 1, t, half(h)], xr.at[dx - 1, t, half(h)],
                      rsx_s.at[it, dx - 1, t, h], rsx_r.at[it, dx - 1, t, h],
                      samples=z * X + (x + dx) % X)

        def zcopy(t, h, d):
            return to(zs.at[t, half(h)], zr.at[d, t, half(h)], rsz_s.at[it, t, h],
                      rsz_r.at[it, d, t, h], samples=me + X - 2 * X * d)

        def ecopy(dx):
            return to(es.at[dx - 1], er.at[dx - 1], rse_s.at[it, dx - 1],
                      rse_r.at[it, dx - 1], samples=peer)

        def term(t, xx, w):
            return chain[last[(t * X + xx) * SB + w]]

        order = []
        a, b = z * 0, z * 0 + Z - 1
        for k in range(Z):
            low_end = (z - a > b - z).astype(jnp.int32)
            order.append(a * low_end + b * (1 - low_end))
            a = a + low_end
            b = b - (1 - low_end)

        def send_x(t, h, dx, extra=False):
            xx = (x + dx) % X

            @pl.loop(0, HS)
            def _(v):
                w = v + h * HS
                total = term(t, xx, w)
                if extra:
                    total = total + er[dx - 1, v].astype(F32)
                xs[dx - 1, t, w] = total.astype(BF16)

            xcopy(t, h, dx).start()

        def send_extra():
            for dx in range(1, X):
                @pl.loop(0, HS)
                def _(v):
                    es[dx - 1, v] = term(zp, (x + dx) % X, v + HS).astype(BF16)

                ecopy(dx).start()

        for k, t in enumerate(order):
            for h in (0, 1):
                for dx in range(1, X):
                    if h == 0:
                        send_x(t, h, dx)
                    elif k < Z - 1:
                        pl.when(t != zp)(lambda t=t, dx=dx: send_x(t, 1, dx))
                    else:
                        ecopy(dx).wait_recv()
                        send_x(t, h, dx, True)
                if k == 0 and h == 0:
                    send_extra()
        for t in order:
            @pl.loop(0, SB)
            def _(w):
                acc[t, w] = term(t, x, w)

        beside()

        def add_x(t, h):
            for dx in range(1, X):
                xcopy(t, h, dx).wait_recv()

            @pl.loop(h * HS, (h + 1) * HS)
            def _(w):
                total = acc[t, w]
                for dx in range(1, X):
                    total = total + xr[dx - 1, t, w].astype(F32)
                acc[t, w] = total

        def add_z(t, h, d):
            zcopy(t, h, d).wait_recv()

            @pl.loop(h * HS, (h + 1) * HS)
            def _(w):
                acc[t, w] = acc[t, w] + zr[d, t, w].astype(F32)

        for k, t in enumerate(order):
            if k == Z - 1:
                late()
            for h in (0, 1):
                if h == 1 and k < Z - 1:
                    pl.when(t != zp)(lambda t=t: add_x(t, 1))
                else:
                    add_x(t, h)
                if k == Z - 1:
                    pl.when(z > 0)(lambda t=t, h=h: add_z(t, h, 0))
                    pl.when(z + 1 < Z)(lambda t=t, h=h: add_z(t, h, 1))
                    continue
                d = (t < z).astype(jnp.int32)
                relay = ((t > z) & (z > 0)) | ((t < z) & (z + 1 < Z))
                pl.when(relay)(lambda t=t, h=h, d=d: add_z(t, h, d))

                @pl.loop(h * HS, (h + 1) * HS)
                def _(w):
                    zs[t, w] = acc[t, w].astype(BF16)

                zcopy(t, h, d).start()
        def drain():
            for t in range(Z):
                for dx in range(1, X):
                    xcopy(t, 0, dx).wait_send()
                    pl.when(t != zp)(lambda t=t, dx=dx: xcopy(t, 1, dx).wait_send())
                for h in (0, 1):
                    pl.when(t != z)(lambda t=t, h=h: zcopy(t, h, 0).wait_send())
            for dx in range(1, X):
                ecopy(dx).wait_send()

        return drain

    def tile_copy(j, m, d, src):
        other = (mine + d) % (2 * n)
        rows = pl.ds(0, 8 * m)
        return to(all_buf.at[j, src, rows], all_buf.at[j, src, rows], ar_s.at[j, d],
                  ar_r.at[j, d], samples=other // 2, features=other % 2)

    def sum_start(j, values):
        for i, v in enumerate(values):
            all_buf[j, mine, pl.ds(8 * i, 8)] = v

        @pl.loop(1, 2 * n)
        def _(d):
            tile_copy(j, len(values), d, mine).start()

    def sum_finish(j, m):
        @pl.loop(1, 2 * n)
        def _(d):
            tile_copy(j, m, d, (mine - d + 2 * n) % (2 * n)).wait_recv()

        @pl.loop(1, 2 * n)
        def _(d):
            tile_copy(j, m, d, mine).wait_send()

        rows = pl.ds(0, 8 * m)
        total = all_buf[j, 0, rows]
        for s in range(1, 2 * n):
            total = total + all_buf[j, s, rows]
        return [jnp.sum(total[8 * i:8 * i + 8], axis=0, keepdims=True) for i in range(m)]

    @pl.loop(0, SB)
    def _(w):
        panel[me * SB + w] = right[w].astype(BF16)

    pl.semaphore_wait(barrier, 2 * n - 1)
    chain[0] = jnp.zeros(chain.shape[1:], F32)
    got = {}

    def first_norm():
        got["own"] = lax.fori_loop(0, SB, lambda w, c: c + fold(right[w] * right[w]), zero)

    gathered = gather(0, first_norm, load.wait)
    norm = ratio = None
    for it in range(ITERS):
        first, final = it == 0, it == ITERS - 1
        direction = right if first else p
        residual = right if first else res
        squares, sent = products(it, ratio, gathered)

        def send_sums():
            own = got["own"]
            if first:
                sum_start(0, [own, squares + lam[...] * own])
            else:
                before = right if it == 1 else p

                def turn(w, carry):
                    v = res[w] + ratio * before[w]
                    p[w] = v
                    return carry + fold(v * v)

                own = lax.fori_loop(0, SB, turn, zero)
                sum_start(2 * it, [squares + lam[...] * own])
            sent()

        def take_sums():
            got["sums"] = sum_finish(2 * it, 2 if first else 1)

        scattered = scatter(it, send_sums, take_sums)
        if first:
            norm = got["sums"][0]
        step = norm / got["sums"][-1]

        def update(w, carry):
            v = direction[w]
            sol[w] = step * v if first else sol[w] + step * v
            new = residual[w] - step * (acc[z, w] + lam[...] * v)
            res[w] = new
            if not final:
                panel[me * SB + w] = new.astype(BF16)
            return carry + fold(new * new)

        sq = lax.fori_loop(0, SB, update, zero)
        if final:
            scattered()
        else:
            def send_norm():
                sum_start(2 * it + 1, [sq])
                scattered()

            def take_norm():
                got["norm"] = sum_finish(2 * it + 1, 1)[0]

            gathered = gather(it + 1, send_norm, take_norm)
            ratio = got["norm"] / norm
            norm = got["norm"]


def img_rows(rb):
    return max(d for d in range(1, 4) if rb % d == 0)


def per_device(n, blocks, block_cols, right_side, lambdas):
    RB, E, B, _ = blocks.shape
    K = right_side.shape[1]
    SB = right_side.shape[0] // B
    X = row_length(n)
    Z = n // X
    slots = (block_cols // (2 * SB) * SB + block_cols % SB).reshape(-1)
    entries = jnp.arange(RB * E, dtype=jnp.int32)
    same = (slots[:, None] == slots[None, :]) & (entries[None, :] < entries[:, None])
    prev = jnp.max(jnp.where(same, entries[None, :] + 1, 0), axis=1)
    hit = slots[None, :] == jnp.arange(n * SB, dtype=jnp.int32)[:, None]
    last = jnp.max(jnp.where(hit, entries[None, :] + 1, 0), axis=1)
    C = RB // img_rows(RB)
    dma = pltpu.SemaphoreType.DMA
    J = 2 * ITERS
    smem = pl.BlockSpec(memory_space=pltpu.SMEM)
    vmem = pl.BlockSpec(memory_space=pltpu.VMEM)
    sol, res = pl.pallas_call(
        functools.partial(kernel, n, X, SB),
        out_shape=[jax.ShapeDtypeStruct((SB, B, K), F32)] * 2,
        in_specs=[smem, smem, smem, pl.BlockSpec(memory_space=pl.ANY), vmem, vmem],
        out_specs=[vmem, vmem],
        scratch_shapes=[
            pltpu.VMEM((RB, E, B, B), BF16),
            pltpu.VMEM((n * SB, B, K), BF16),
            pltpu.VMEM((RB, B, K), F32),
            pltpu.VMEM((RB, B, K), F32),
            pltpu.VMEM((RB * E + 1, B, K), F32),
            pltpu.VMEM((Z, SB, B, K), F32),
            pltpu.VMEM((X - 1, Z, SB, B, K), BF16),
            pltpu.VMEM((X - 1, Z, SB, B, K), BF16),
            pltpu.VMEM((Z, SB, B, K), BF16),
            pltpu.VMEM((2, Z, SB, B, K), BF16),
            pltpu.VMEM((X - 1, SB // 2, B, K), BF16),
            pltpu.VMEM((X - 1, SB // 2, B, K), BF16),
            pltpu.VMEM((SB, B, K), F32),
            pltpu.VMEM((RB, B, K), F32),
            pltpu.VMEM((J, 2 * n, 16, K), F32),
            dma,
            dma((ITERS, 2, Z, 2)), dma((ITERS, Z, 2)),
            dma((ITERS, X - 1, Z, 2)), dma((ITERS, X - 1, Z, 2)),
            dma((ITERS, X - 1)), dma((ITERS, X - 1)),
            dma((ITERS, C)), dma((ITERS, C)),
            dma((ITERS, X - 1, Z, 2)), dma((ITERS, X - 1, Z, 2)),
            dma((ITERS, Z, 2)), dma((ITERS, 2, Z, 2)),
            dma((ITERS, X - 1)), dma((ITERS, X - 1)),
            dma((J, 2 * n)), dma((J, 2 * n)),
        ],
        compiler_params=pltpu.CompilerParams(
            collective_id=0, has_side_effects=True, vmem_limit_bytes=60 * 2**20),
    )(slots, prev, last, blocks, right_side.reshape(SB, B, K), lambdas.reshape(1, K))
    return sol.reshape(right_side.shape), res.reshape(right_side.shape)


def solution(mesh):
    in_specs = (
        P(("groups", "samples"), "features", None, None),
        P(("groups", "samples"), "features"),
        P(("groups", "samples", "features"), None),
        P(),
    )
    out_specs = (
        P(("groups", "samples", "features"), None),
        P(("groups", "samples", "features"), None),
    )
    return jax.shard_map(
        functools.partial(per_device, mesh.shape["samples"]),
        mesh=mesh, in_specs=in_specs, out_specs=out_specs, check_vma=False,
    )
```
